256 devices in a mesh: pair: 16 (over y, z_lo, core), virt: 16 (over z_hi, x).
Axes of the slice: x: 4, y: 4, z: 8 (z_hi: 4, z_lo: 2; z = z_hi * 2 + z_lo), core: 2. Of those that a mesh axis runs over, the one named last changes fastest.
Arguments:
- amplitudes: bfloat16 [24576, 4096], P('pair', 'virt'), may hold values from -6 to 6
- amp_map: int32 [192, 32], P('pair', 'virt'), may hold values 0 or 1
- integral_tiles: bfloat16 [128, 16, 128, 128], P('virt', 'pair'), may hold values from -0.25 to 0.25
- integral_cols: int32 [128, 16], P('virt'), may hold values from 0 to 31, all different within a row
- live_slots: int32 [128], P('virt'), may hold values from 1 to 16, 1280 in all
- pair_orbitals: int32 [2, 24576], P(None, 'pair'), may hold values from 0 to 1499
- virtual_pairs: int32 [2, 16384], P(None, 'virt'), may hold values from 0 to 11999
- occupied_energy: float32 [1500], replicated, may hold values from -1.5 to -0.3
- virtual_energy: float32 [12000], replicated, may hold values from 0.2 to 3
Outputs:
- ladder_update: bfloat16 [24576, 16384], P('pair', 'virt')
The draws below stay inside these ranges and needn't reach their ends.
Inputs may be any that keep to these rules, and one draw needn't show every extreme that they name: `integral_cols`: row k lists 16 different amplitude column tiles; every column tile is listed by some row. Slot s of virtual-pair tile k is used when s < live_slots[k]; some tile uses all 16.
All inputs are finite; a program needn't handle non-finite values. No bound on the sum of `amp_map` or of `live_slots` on one device may be relied on, other than what follows from the above.
Results may differ from the reference program's by a relative error of at most 0.001.
Values may be sent and summed in bfloat16 or wider, within the bound.
No kernel may reach another device: no remote copies, remote signals or barrier semaphores. Data moves between devices by JAX's collectives and lax.ppermute only.
A program may use at most 128 MiB of HBM per device.

```python
import math
import jax
import jax.numpy as jnp
import numpy as np
from jax import lax

TILE = 128
NOCC = 1500
NVIRT = 12000
KV = 16
NPT = 192
NPAIR = 24576
NCD = 32
NAB = 128


def set_ends(values, rng, smallest, high):
    index_at = [jax.random.randint(jax.random.fold_in(rng, axis), (), 0, length) for axis, length in enumerate(values.shape)]
    main_axis = values.shape.index(max(values.shape))
    next_to = index_at[:main_axis] + [(index_at[main_axis] + 1) % values.shape[main_axis]] + index_at[main_axis + 1:]
    return values.at[tuple(index_at)].set(smallest).at[tuple(next_to)].set(high)


def block_scale(stream_key, extent, shards, smallest, largest):
    gain, own = 1.0, jax.random.fold_in(stream_key, 6)
    for dim, parts in shards:
        steps = jnp.exp(jax.random.uniform(jax.random.fold_in(own, dim), (parts,), jnp.float32, smallest / len(shards), largest / len(shards)))
        gain = gain * jnp.repeat(steps, extent[dim] // parts).reshape([-1 if axis == dim else 1 for axis in range(len(extent))])
    return gain


def distinct(rng, rows, number_of, top, lift):
    sequence = jax.random.permutation(jax.random.fold_in(rng, 1), number_of)
    boost = sequence
    for power in range(3):
        boost = boost * boost // number_of
    boost = boost * lift // number_of
    chance = jax.random.randint(jax.random.fold_in(rng, 2), (rows, number_of), 0, 4096) + boost
    sure = jax.random.permutation(jax.random.fold_in(rng, 3), rows)[jnp.arange(number_of) % rows]
    chance = jnp.where(jnp.arange(rows)[:, None] == sure[None, :], 1 << 14, chance)
    score = chance * number_of + jnp.arange(number_of)
    return lax.top_k(score.astype(jnp.int32), top)[1].astype(jnp.int32)


def profile(count, total, most, lean):
    loads = [(1 << 20) // math.isqrt(standing ** lean) + 1 for standing in range(2, count + 1)]
    spare, given = total - most - (count - 1), [1] * (count - 1)
    while spare > 0:
        movable = [i for i in range(count - 1) if given[i] < most]
        pool, left = sum([loads[i] for i in movable]), spare
        for i in movable:
            more = min(most - given[i], max(1, left * loads[i] // pool), spare)
            given[i] = given[i] + more
            spare = spare - more
    return np.array([most] + given)


def ragged(key, amount, total, most, slope):
    if amount == 2:
        one = jax.random.randint(key, (), max(1, total - most), min(most, total - 1) + 1)
        return jnp.stack([one, total - one])
    tallies = jnp.asarray(profile(amount, total, most, slope), jnp.int32)
    twos = (amount - 1) // 2
    donor, sink = tallies[1:1 + 2 * twos:2], tallies[2:2 + 2 * twos:2]
    room = jnp.minimum(donor - 1, most - sink)
    passed = jax.random.randint(jax.random.fold_in(key, 1), (twos,), 0, 1 << 20) % (room + 1)
    tallies = tallies.at[1:1 + 2 * twos:2].set(donor - passed).at[2:2 + 2 * twos:2].set(sink + passed)
    return tallies[jax.random.permutation(jax.random.fold_in(key, 2), amount)]


def noise(own_key, shape, width, bound, pieces=(), held_as=jnp.bfloat16):
    array = jax.random.normal(own_key, shape, jnp.float32) * width
    if len(pieces) > 0:
        array = block_scale(own_key, shape, pieces, -0.22, 0.18) * array
    return jnp.clip(array, min=-bound, max=bound).astype(held_as)


def setup_inputs(seed: int = 0) -> dict:
    key_list = jax.random.split(jax.random.key(seed), 10)
    amplitudes = noise(key_list[0], (NPAIR, NCD * TILE), 1.0, 6.0, ((0, 16), (1, 16)))
    amp_map = set_ends((jax.random.randint(key_list[1], (NPT, NCD), 0, 2) < 1).astype(jnp.int32), jax.random.fold_in(key_list[1], 1), 0, 1)
    integral_tiles = noise(key_list[2], (NAB, KV, TILE, TILE), (KV * TILE // 4) ** -0.5, 0.25, ((0, 16), (1, 16)))
    integral_cols = distinct(key_list[3], NAB, NCD, KV, 0)
    live_slots = ragged(key_list[4], NAB, NAB * KV * 5 // 8, KV, 2).astype(jnp.int32)
    pair_orbitals = set_ends(jax.random.randint(key_list[5], (2, NPAIR), 0, NOCC), jax.random.fold_in(key_list[5], 1), 0, NOCC - 1).astype(jnp.int32)
    virtual_pairs = set_ends(jax.random.randint(key_list[6], (2, NAB * TILE), 0, NVIRT), jax.random.fold_in(key_list[6], 1), 0, NVIRT - 1).astype(jnp.int32)
    occupied_energy = jnp.clip(jax.random.uniform(key_list[7], (NOCC,), jnp.float32, -1.5, -0.3), -1.5, -0.3)
    virtual_energy = jnp.clip(jax.random.uniform(key_list[8], (NVIRT,), jnp.float32, 0.2, 3.0), 0.2, 3.0)
    return dict(amplitudes=amplitudes, amp_map=amp_map, integral_tiles=integral_tiles, integral_cols=integral_cols, live_slots=live_slots, pair_orbitals=pair_orbitals, virtual_pairs=virtual_pairs, occupied_energy=occupied_energy, virtual_energy=virtual_energy)


def one_tile(masked, packed):
    weights_k, cols_k = packed
    picked = jnp.take(masked, cols_k, axis=1)
    return jnp.einsum("rsx,sxy->ry", picked.astype(jnp.float32), weights_k.astype(jnp.float32))


def reference(amplitudes, amp_map, integral_tiles, integral_cols, live_slots, pair_orbitals, virtual_pairs, occupied_energy, virtual_energy):
    tiled = amplitudes.reshape(NPT, TILE, NCD, TILE)
    masked = (tiled * amp_map.astype(jnp.bfloat16)[:, None, :, None]).reshape(NPAIR, NCD, TILE)
    slot_live = jnp.arange(KV, dtype=jnp.int32)[None, :] < live_slots[:, None]
    weights = jnp.where(slot_live[:, :, None, None], integral_tiles, jnp.zeros((), jnp.bfloat16))
    ladder = lax.map(lambda packed: one_tile(masked, packed), (weights, integral_cols))
    ladder = jnp.transpose(ladder, (1, 0, 2)).reshape(NPAIR, NAB * TILE)
    pair_energy = occupied_energy[pair_orbitals[0]] + occupied_energy[pair_orbitals[1]]
    virtual_sum = virtual_energy[virtual_pairs[0]] + virtual_energy[virtual_pairs[1]]
    return (ladder / (virtual_sum[None, :] - pair_energy[:, None])).astype(jnp.bfloat16)
```

```python
import functools

import jax
import jax.numpy as jnp
import numpy as np
from jax import lax
from jax.experimental import pallas as pl
from jax.experimental.pallas import tpu as pltpu
from jax.sharding import PartitionSpec as P

ANY = pl.BlockSpec(memory_space=pl.ANY)
SMEM = pl.BlockSpec(memory_space=pltpu.SMEM)
VMEM = pl.BlockSpec(memory_space=pltpu.VMEM)
VMEM_LIMIT = 50 * 1024 * 1024
RING = 4
RING_ROWS = 832
GROUP = 4


def slot_table():
    table = np.zeros((16, 16), np.int32)
    for pair in range(16):
        y, zlo, core = pair // 4, pair // 2 % 2, pair % 2
        for local in range(16):
            which, dy, other = local // 8, local % 8 // 2, local % 2
            table[pair, local] = (y - dy) % 4 * 4 + (zlo ^ other) * 2 + (core ^ which)
    return table


def column_table(keys):
    return np.array(
        [
            [(virt // RING - dz) % RING * RING + (virt % RING - dx) % RING for dz, dx in keys]
            for virt in range(RING * RING)
        ],
        np.int32,
    )


def barrier(*arrays):
    return lax.optimization_barrier(arrays)


def after(array, *first):
    return lax.optimization_barrier((array,) + first)[0]


def virt_shift(array, dz, dx):
    pairs = [
        (z * RING + x, (z + dz) % RING * RING + (x + dx) % RING)
        for z in range(RING)
        for x in range(RING)
    ]
    return lax.ppermute(array, "virt", pairs)


def pair_shift(array, dy):
    return lax.ppermute(array, "pair", [(i, (i + 4 * dy) % 16) for i in range(16)])


def pair_swap(array, bit):
    return lax.ppermute(array, "pair", [(i, i ^ bit) for i in range(16)])


def table_lookup(table, index):
    rows = -(-table.shape[0] // 128)
    padded = jnp.zeros((rows * 128,), jnp.float32).at[: table.shape[0]].set(table).reshape(rows, 128)
    chosen = (index[:, None] // 128 == jnp.arange(rows, dtype=jnp.int32)[None, :]).astype(jnp.float32)
    lines = jnp.dot(chosen, padded, precision=lax.Precision.HIGHEST)
    lane = index[:, None] % 128 == jnp.arange(128, dtype=jnp.int32)[None, :]
    return jnp.sum(jnp.where(lane, lines, 0.0), axis=1)


def mask_kernel(amp_map, amplitudes, own, sent):
    split = own.shape[0]
    for tile in range(amp_map.shape[0]):
        for column in range(amp_map.shape[1]):
            keep = amp_map[tile, column].astype(jnp.float32).astype(jnp.bfloat16)
            lanes = slice(column * 128, column * 128 + 128)
            first, last = tile * 128, tile * 128 + 128
            middle = min(max(split, first), last)
            if first < middle:
                own[first:middle, lanes] = amplitudes[first:middle, lanes] * keep
            if middle < last:
                sent[middle - split : last - split, lanes] = amplitudes[middle:last, lanes] * keep


def mask(amplitudes, amp_map, rows):
    count, columns = amplitudes.shape
    return pl.pallas_call(
        mask_kernel,
        in_specs=[SMEM, VMEM],
        out_specs=[VMEM, VMEM],
        out_shape=[
            jax.ShapeDtypeStruct((rows, columns), jnp.bfloat16),
            jax.ShapeDtypeStruct((count - rows, columns), jnp.bfloat16),
        ],
    )(amp_map, amplitudes)


def weights_kernel(slots, cols, live, mine, theirs, out):
    tile = pl.program_id(0)
    out[...] = jnp.zeros_like(out)
    for local in range(16):
        slot = slots[local]
        source = mine if local < 8 else theirs

        @pl.when(slot < live[tile])
        def _(local=local, slot=slot, source=source):
            row = pl.multiple_of(cols[tile, slot] * 128, 128)
            out[pl.ds(row, 128), :] = source[0, local % 8]


def dense_weights(slots, cols, live, mine, theirs):
    tiles = cols.shape[0]
    block = pl.BlockSpec((1, 8, 128, 128), lambda k: (k, 0, 0, 0))
    return pl.pallas_call(
        weights_kernel,
        grid=(tiles,),
        in_specs=[SMEM] * 3 + [block] * 2,
        out_specs=pl.BlockSpec((4096, 128), lambda k: (0, k)),
        out_shape=jax.ShapeDtypeStruct((4096, tiles * 128), jnp.bfloat16),
        cost_estimate=pl.CostEstimate(flops=0, bytes_accessed=tiles * 24 * 2**16, transcendentals=0),
        compiler_params=pltpu.CompilerParams(vmem_limit_bytes=VMEM_LIMIT),
    )(slots, cols, live, mine, theirs)


def matmul_kernel(plan, piece_count, rows, row0, has_total, final, has_base, *refs):
    refs = list(refs)
    where, weights = refs[:2]
    pieces = refs[2 : 2 + piece_count]
    rest = refs[2 + len(pieces) :]
    total_in = rest.pop(0) if has_total else None
    if final:
        virtual_sum, pair_energy = rest.pop(0), rest.pop(0)
    if has_base:
        rest.pop(0)
    out = rest.pop(0)
    held, wheld, total = rest[:3]
    held_sem, w_sem, total_sem, out_sem = rest[3:7]
    staged = rest[7] if final else None
    count = len(plan)
    if has_total:
        load_total = pltpu.make_async_copy(total_in, total, total_sem)
        load_total.start()
    for j, parts in enumerate(plan):
        for piece, first, start, size in parts:
            source = pieces[piece]
            source = source.at[first] if len(source.shape) == 3 else source.at[pl.ds(first, size)]
            pltpu.make_async_copy(
                source, held.at[pl.ds(start, size), pl.ds(j * 256, 256)], held_sem.at[j]
            ).start()
        pltpu.make_async_copy(
            weights.at[pl.ds(pl.multiple_of(where[j] * 256, 256), 256)],
            wheld.at[pl.ds(j * 256, 256)],
            w_sem.at[j],
        ).start()
    if has_total:
        load_total.wait()
    for group in range(0, count, GROUP):
        last = min(group + GROUP, count)
        for j in range(group, last):
            slot = held.at[:, pl.ds(j * 256, 256)]
            pltpu.make_async_copy(slot, slot, held_sem.at[j]).wait()
            wslot = wheld.at[pl.ds(j * 256, 256)]
            pltpu.make_async_copy(wslot, wslot, w_sem.at[j]).wait()
        first = group == 0 and not has_total
        ends = last == count

        product = jnp.dot(
            held[:, group * 256 : last * 256],
            wheld[group * 256 : last * 256, :],
            preferred_element_type=jnp.float32,
        )
        if not first:
            product = total[...] + product
        if ends and final:
            staged[...] = (product / (virtual_sum[...] - pair_energy[...])).astype(jnp.bfloat16)
        else:
            total[...] = product
    if final:
        store = pltpu.make_async_copy(staged, out.at[pl.ds(row0, rows)], out_sem)
    else:
        store = pltpu.make_async_copy(total, out, out_sem)
    store.start()
    store.wait()


def block_matmul(where, weights, plan, pieces, rows, row0=0, all_rows=0, total=None, energies=None, base=None):
    columns = weights.shape[1]
    count = len(plan)
    final = energies is not None
    operands = [where, weights] + list(pieces)
    specs = [SMEM] + [ANY] * (1 + len(pieces))
    if total is not None:
        operands.append(total)
        specs.append(ANY)
    if final:
        operands += list(energies)
        specs += [VMEM, VMEM]
    aliases = {}
    if base is not None:
        aliases = {len(operands): 0}
        operands.append(base)
        specs.append(ANY)
    shape = (all_rows, columns) if final else (rows, columns)
    kind = jnp.bfloat16 if final else jnp.float32
    scratch = [
        pltpu.VMEM((rows, count * 256), jnp.bfloat16),
        pltpu.VMEM((count * 256, columns), jnp.bfloat16),
        pltpu.VMEM((rows, columns), jnp.float32),
        pltpu.SemaphoreType.DMA((count,)),
        pltpu.SemaphoreType.DMA((count,)),
        pltpu.SemaphoreType.DMA,
        pltpu.SemaphoreType.DMA,
    ]
    if final:
        scratch.append(pltpu.VMEM((rows, columns), jnp.bfloat16))
    return pl.pallas_call(
        functools.partial(matmul_kernel, plan, len(pieces), rows, row0, total is not None, final, base is not None),
        in_specs=specs,
        out_specs=ANY,
        out_shape=jax.ShapeDtypeStruct(shape, kind),
        scratch_shapes=scratch,
        input_output_aliases=aliases,
        cost_estimate=pl.CostEstimate(
            flops=2 * rows * count * 256 * columns,
            bytes_accessed=(rows + columns) * count * 512 + rows * columns * 8,
            transcendentals=0,
        ),
        compiler_params=pltpu.CompilerParams(vmem_limit_bytes=VMEM_LIMIT),
    )(*operands)


def per_device(
    amplitudes,
    amp_map,
    integral_tiles,
    integral_cols,
    live_slots,
    pair_orbitals,
    virtual_pairs,
    occupied_energy,
    virtual_energy,
):
    row_count = amplitudes.shape[0]
    rows = RING_ROWS
    gather_rows = row_count - rows
    half = rows // 2
    own, sent = mask(amplitudes, amp_map, rows)

    pair = lax.axis_index("pair")
    virt = lax.axis_index("virt")

    gathered = lax.all_gather(sent, "virt", axis=0)

    two = jnp.concatenate([integral_tiles, pair_swap(integral_tiles, 2)], axis=1)
    own, two = barrier(own, two)
    x1, x3 = virt_shift(own, 0, 1), virt_shift(own, 0, -1)
    z1, z3, x1, x3, x2a, x2b, y1, y2, y3 = barrier(
        virt_shift(own, 1, 0),
        virt_shift(own, -1, 0),
        x1,
        x3,
        virt_shift(x1[:half], 0, 1),
        virt_shift(x3[half:], 0, -1),
        pair_shift(two, 1),
        pair_shift(two, 2),
        pair_shift(two, -1),
    )
    mine = jnp.concatenate([two, y1, y2, y3], axis=1)
    near = jnp.concatenate([z1, z3])
    z2a, z2b, right, left, theirs = barrier(
        virt_shift(z1[:half], 1, 0),
        virt_shift(z3[half:], -1, 0),
        virt_shift(near, 0, 1),
        virt_shift(near, 0, -1),
        pair_swap(mine, 1),
    )
    weights = dense_weights(jnp.asarray(slot_table())[pair], integral_cols, live_slots, mine, theirs)

    right2, left2 = barrier(
        virt_shift(jnp.concatenate([right[:rows], z2a, z2b]), 0, 1),
        virt_shift(jnp.concatenate([left[rows:], z2a, z2b]), 0, -1),
    )
    def whole(array, first=0):
        return [(array, first, 0, rows)]

    def halves(low, low_first, high, high_first):
        return [(low, low_first, 0, half), (high, high_first, half, half)]

    block = {
        (0, 0): whole(own),
        (1, 0): whole(z1),
        (3, 0): whole(z3),
        (0, 1): whole(x1),
        (0, 3): whole(x3),
        (2, 0): halves(z2a, 0, z2b, 0),
        (0, 2): halves(x2a, 0, x2b, 0),
        (1, 1): whole(right),
        (3, 1): whole(right, rows),
        (1, 3): whole(left),
        (3, 3): whole(left, rows),
    }

    pair_orbitals, virtual_pairs = after(pair_orbitals, z1), after(virtual_pairs, z1)
    occupied = table_lookup(occupied_energy, pair_orbitals.reshape(-1)).reshape(2, -1)
    virtual = table_lookup(virtual_energy, virtual_pairs.reshape(-1)).reshape(2, -1)
    pair_energy = (occupied[0] + occupied[1])[:, None]
    virtual_sum = (virtual[0] + virtual[1])[None, :]

    def multiply(keys, **options):
        where = jnp.asarray(column_table(keys))[virt]
        plan, pieces, seen = [], [], {}
        for key in keys:
            parts = []
            for array, first, start, size in block[key]:
                if id(array) not in seen:
                    seen[id(array)] = len(pieces)
                    pieces.append(array)
                parts.append((seen[id(array)], first, start, size))
            plan.append(tuple(parts))
        return block_matmul(where, weights, tuple(plan), pieces, rows, **options)

    early = [(0, 0), (1, 0), (3, 0), (0, 1), (0, 3), (2, 0), (0, 2), (1, 1), (1, 3), (3, 1), (3, 3)]
    late = [(1, 2), (3, 2), (2, 1), (2, 3)]
    total = multiply(early)
    right2, left2, total = barrier(right2, left2, total)
    right3 = virt_shift(right2[rows : rows + half], 0, 1)
    left3 = virt_shift(left2[rows + half :], 0, -1)
    block.update(
        {
            (1, 2): whole(right2),
            (3, 2): whole(left2),
            (2, 1): halves(right2, rows, right2, rows + half),
            (2, 3): halves(left2, rows, left2, rows + half),
            (2, 2): halves(right3, 0, left3, 0),
        }
    )
    total = multiply(late, total=total)
    result = block_matmul(
        jnp.arange(16, dtype=jnp.int32),
        weights,
        tuple(((0, v, 0, gather_rows),) for v in range(16)),
        [gathered],
        gather_rows,
        row0=rows,
        all_rows=row_count,
        energies=(virtual_sum, pair_energy[rows:]),
    )
    return multiply(
        [(2, 2)],
        total=total,
        energies=(virtual_sum, pair_energy[:rows]),
        all_rows=row_count,
        base=result,
    )


def solution(mesh):
    placed = (
        P("pair", "virt"),
        P("pair", "virt"),
        P("virt", "pair", None, None),
        P("virt", None),
        P("virt"),
        P(None, "pair"),
        P(None, "virt"),
        P(),
        P(),
    )
    return jax.shard_map(
        per_device, mesh=mesh, in_specs=placed, out_specs=P("pair", "virt"), check_vma=False
    )
```

```python
import functools

import jax
import jax.numpy as jnp
import numpy as np
from jax import lax
from jax.experimental import pallas as pl
from jax.experimental.pallas import tpu as pltpu
from jax.sharding import PartitionSpec as P

ANY = pl.BlockSpec(memory_space=pl.ANY)
SMEM = pl.BlockSpec(memory_space=pltpu.SMEM)
VMEM = pl.BlockSpec(memory_space=pltpu.VMEM)
EARLY_VMEM = 27 * 1024 * 1024
LATE_VMEM = 11 * 1024 * 1024
RING = 4
CROSS_ROWS = 320
GROUP = 4
ORDER = (
    [(2, 0), (2, 1), (2, 3)]
    + [(0, 0), (0, 1), (0, 3), (1, 0), (3, 0), (1, 1), (1, 3), (3, 1), (3, 3), (1, 2), (3, 2)]
    + [(0, 2), (2, 2)]
)
TAIL_SLOTS = (0, 1, 2, 15, 14)


def slot_table():
    table = np.zeros((16, 16), np.int32)
    for pair in range(16):
        y, zlo, core = pair // 4, pair // 2 % 2, pair % 2
        for local in range(16):
            far, swapped, near = local // 8, local // 4 % 2, local // 2 % 2
            other_y = (y + 2 * far) % 4 ^ near
            table[pair, local] = other_y * 4 + (zlo ^ local % 2) * 2 + (core ^ swapped)
    return table


def order_table():
    table = np.zeros((16, 16), np.int32)
    for virt in range(RING * RING):
        for place, (dz, dx) in enumerate(ORDER):
            table[virt, (virt // RING - dz) % RING * RING + (virt % RING - dx) % RING] = place
    return table


def barrier(*arrays):
    return lax.optimization_barrier(arrays)


def after(array, *first):
    return lax.optimization_barrier((array,) + first)[0]


def virt_shift(array, dz, dx):
    pairs = [
        (z * RING + x, (z + dz) % RING * RING + (x + dx) % RING)
        for z in range(RING)
        for x in range(RING)
    ]
    return lax.ppermute(array, "virt", pairs)


def pair_swap(array, bit):
    return lax.ppermute(array, "pair", [(i, i ^ bit) for i in range(16)])


def opposite_y(array):
    return lax.ppermute(array, "pair", [(i, (i + 8) % 16) for i in range(16)])


def table_lookup(table, index):
    rows = -(-table.shape[0] // 128)
    padded = jnp.zeros((rows * 128,), jnp.float32).at[: table.shape[0]].set(table).reshape(rows, 128)
    chosen = (index[:, None] // 128 == jnp.arange(rows, dtype=jnp.int32)[None, :]).astype(jnp.float32)
    lines = jnp.dot(chosen, padded, precision=lax.Precision.HIGHEST)
    lane = index[:, None] % 128 == jnp.arange(128, dtype=jnp.int32)[None, :]
    return jnp.sum(jnp.where(lane, lines, 0.0), axis=1)


def mask_kernel(whole, amp_map, amplitudes, masked, front):
    for tile in range(amp_map.shape[1]):
        for column in range(amp_map.shape[0]):
            keep = amp_map[column, tile].astype(jnp.float32).astype(jnp.bfloat16)
            block = (slice(tile * 128, tile * 128 + 128), slice(column * 128, column * 128 + 128))
            masked[block] = amplitudes[block] * keep
    front[...] = masked[:whole]


def mask(amplitudes, amp_map, whole):
    rows, columns = amplitudes.shape
    return pl.pallas_call(
        functools.partial(mask_kernel, whole),
        in_specs=[SMEM, VMEM],
        out_specs=[VMEM] * 2,
        out_shape=[jax.ShapeDtypeStruct((n, columns), jnp.bfloat16) for n in (rows, whole)],
    )(amp_map.T, amplitudes)


def pack_kernel(plan, count, *refs):
    sem = refs[-1]
    copies = []
    for target, parts in zip(refs[count:-1], plan):
        at = 0
        for source, first, size in parts:
            copies.append(
                pltpu.make_async_copy(
                    refs[source].at[pl.ds(first, size)], target.at[pl.ds(at, size)], sem.at[len(copies)]
                )
            )
            at += size
    for copy in copies:
        copy.start()
    for copy in copies:
        copy.wait()


def pack(*lists):
    arrays, plan, shapes = [], [], []
    for parts in lists:
        made = []
        for array, first, size in parts:
            known = [i for i, other in enumerate(arrays) if other is array]
            if not known:
                arrays.append(array)
            made.append((known[0] if known else len(arrays) - 1, first, size))
        plan.append(made)
        shapes.append((sum(size for _, _, size in parts),) + parts[0][0].shape[1:])
    return pl.pallas_call(
        functools.partial(pack_kernel, plan, len(arrays)),
        in_specs=[ANY] * len(arrays),
        out_specs=[VMEM] * len(shapes),
        out_shape=[jax.ShapeDtypeStruct(shape, jnp.bfloat16) for shape in shapes],
        scratch_shapes=[pltpu.SemaphoreType.DMA((sum(len(parts) for parts in plan),))],
        cost_estimate=pl.CostEstimate(
            flops=0, bytes_accessed=sum(2 * int(np.prod(shape)) for shape in shapes), transcendentals=0
        ),
    )(*arrays)


def segment_dot(held, arrived, weights, first_slot, count):
    product = None
    for group in range(0, count, GROUP):
        last = min(group + GROUP, count)
        for j in range(group, last):
            arrived(j)
        part = jnp.dot(
            held[:, group * 256 : last * 256],
            weights[(first_slot + group) * 256 : (first_slot + last) * 256, :],
            preferred_element_type=jnp.float32,
        )
        product = part if product is None else product + part
    return product


def start_blocks(plan, pieces, held, held_sem):
    for s, (_, rows, _, parts) in enumerate(plan):
        for j, (piece, first) in enumerate(parts):
            pltpu.make_async_copy(
                pieces[piece].at[pl.ds(first, rows)],
                held[s].at[:, pl.ds(j * 256, 256)],
                held_sem[s].at[j],
            ).start()


def block_waiter(held, sem):
    def wait(j):
        slot = held.at[:, pl.ds(j * 256, 256)]
        pltpu.make_async_copy(slot, slot, sem.at[j]).wait()

    return wait


def early_kernel(plan, tile_count, piece_count, where, cols, live, *refs):
    sources, refs = refs[:tile_count], refs[tile_count:]
    pieces = refs[:piece_count]
    total, tail, weights, tiles, tile_sem = refs[piece_count : piece_count + 5]
    rest = refs[piece_count + 5 :]
    held, held_sem = rest[: len(plan)], rest[len(plan) :]
    slots = tiles.shape[0]
    each = slots // tile_count
    loads = [
        pltpu.make_async_copy(source, tiles.at[pl.ds(i * each, each)], tile_sem.at[i])
        for i, source in enumerate(sources)
    ]
    for load in loads:
        load.start()
    start_blocks(plan, pieces, held, held_sem)
    weights[...] = jnp.zeros_like(weights)
    for load in loads:
        load.wait()
    for k in range(cols.shape[0]):

        def place(local, carry, k=k):
            slot = where[local]

            @pl.when(slot < live[k])
            def _():
                column = cols[k, slot]
                row = where[slots + column // 2] * 256 + column % 2 * 128
                weights[pl.ds(pl.multiple_of(row, 128), 128), k * 128 : k * 128 + 128] = tiles[local, k]

            return carry

        lax.fori_loop(0, slots, place, 0)
    for i, slot in enumerate(TAIL_SLOTS):
        tail[i * 256 : i * 256 + 256, :] = weights[slot * 256 : slot * 256 + 256, :]
    for s, (first_row, rows, first_slot, parts) in enumerate(plan):
        total[first_row : first_row + rows, :] = segment_dot(
            held[s], block_waiter(held[s], held_sem[s]), weights, first_slot, len(parts)
        )


def late_kernel(plan, piece_count, weights, total, virtual_sum, pair_energy, *refs):
    pieces = refs[:piece_count]
    out, staged, out_sem = refs[piece_count : piece_count + 3]
    rest = refs[piece_count + 3 :]
    held, held_sem = rest[: len(plan)], rest[len(plan) :]
    start_blocks(plan, pieces, held, held_sem)
    stores = []
    for s, (first_row, rows, first_slot, parts) in enumerate(plan):
        span = slice(first_row, first_row + rows)
        product = total[span, :] + segment_dot(
            held[s], block_waiter(held[s], held_sem[s]), weights, first_slot, len(parts)
        )
        staged[span, :] = (product / (virtual_sum[...] - pair_energy[span, :])).astype(jnp.bfloat16)
        store = pltpu.make_async_copy(
            staged.at[pl.ds(first_row, rows)], out.at[pl.ds(first_row, rows)], out_sem.at[s]
        )
        store.start()
        stores.append(store)
    for store in stores:
        store.wait()


def block_scratch(plan):
    held = [pltpu.VMEM((rows, len(parts) * 256), jnp.bfloat16) for _, rows, _, parts in plan]
    return held + [pltpu.SemaphoreType.DMA((len(parts),)) for _, _, _, parts in plan]


def cost(plan, columns, extra):
    work = sum(rows * len(parts) for _, rows, _, parts in plan)
    return pl.CostEstimate(flops=2 * work * 256 * columns, bytes_accessed=work * 512 + extra, transcendentals=0)


def early_matmul(where, cols, live, tiles, plan, pieces):
    columns = cols.shape[0] * 128
    all_rows = sum(rows for _, rows, _, _ in plan)
    return pl.pallas_call(
        functools.partial(early_kernel, plan, len(tiles), len(pieces)),
        in_specs=[SMEM] * 3 + [ANY] * (len(tiles) + len(pieces)),
        out_specs=[VMEM, VMEM],
        out_shape=[
            jax.ShapeDtypeStruct((all_rows, columns), jnp.float32),
            jax.ShapeDtypeStruct((len(TAIL_SLOTS) * 256, columns), jnp.bfloat16),
        ],
        scratch_shapes=[
            pltpu.VMEM((16 * 256, columns), jnp.bfloat16),
            pltpu.VMEM((16,) + tiles[0].shape[1:], jnp.bfloat16),
            pltpu.SemaphoreType.DMA((len(tiles),)),
        ]
        + block_scratch(plan),
        cost_estimate=cost(plan, columns, 16 * 2**20),
        compiler_params=pltpu.CompilerParams(vmem_limit_bytes=EARLY_VMEM),
    )(where, cols, live, *tiles, *pieces)


def late_matmul(weights, total, energies, plan, pieces):
    rows, columns = total.shape
    return pl.pallas_call(
        functools.partial(late_kernel, plan, len(pieces)),
        in_specs=[VMEM] * 4 + [ANY] * len(pieces),
        out_specs=ANY,
        out_shape=jax.ShapeDtypeStruct((rows, columns), jnp.bfloat16),
        scratch_shapes=[
            pltpu.VMEM((rows, columns), jnp.bfloat16),
            pltpu.SemaphoreType.DMA((len(plan),)),
        ]
        + block_scratch(plan),
        cost_estimate=cost(plan, columns, 12 * 2**20),
        compiler_params=pltpu.CompilerParams(vmem_limit_bytes=LATE_VMEM),
    )(weights, total, *energies, *pieces)


def per_device(
    amplitudes,
    amp_map,
    integral_tiles,
    integral_cols,
    live_slots,
    pair_orbitals,
    virtual_pairs,
    occupied_energy,
    virtual_energy,
):
    row_count = amplitudes.shape[0]
    cross = CROSS_ROWS
    part = (row_count - cross) // 2
    whole = row_count - cross
    own, front = mask(amplitudes, amp_map, whole)
    pair = lax.axis_index("pair")
    virt = lax.axis_index("virt")

    spots = np.concatenate(
        [np.repeat(slot_table(), RING * RING, axis=0), np.tile(order_table(), (16, 1))], axis=1
    )
    where = jnp.asarray(spots)[pair * (RING * RING) + virt]

    have = {(0, 0, "p"): (own, 0), (0, 0, "q"): (own, part), (0, 0, "b"): (own, whole)}
    size = {"p": part, "q": part, "b": cross}

    def cut(*lists):
        return pack(*[[have[key] + (size[key[2]],) for key in keys] for keys in lists])

    def arrive(array, keys, dz, dx):
        at = 0
        for z, x, s in keys:
            have[(z + dz) % RING, (x + dx) % RING, s] = (array, at)
            at += size[s]

    def send(array, dz, dx, keys):
        array = virt_shift(array, dz, dx)
        arrive(array, keys, dz, dx)
        return array

    def named(names, z, x):
        return [(z, x, s) for s in names]

    tiles = integral_tiles.reshape((1, integral_tiles.shape[0]) + integral_tiles.shape[2:])
    partner = pair_swap(tiles, 2)
    own, front, partner = barrier(own, front, partner)
    have.update({(0, 0, "p"): (own, 0), (0, 0, "q"): (own, part), (0, 0, "b"): (own, whole)})
    (two,) = pack([(tiles, 0, 1), (partner, 0, 1)])

    z1 = send(front, 1, 0, named("pq", 0, 0))
    z3 = send(front, -1, 0, named("pq", 0, 0))
    x1 = send(own, 0, 1, named("pqb", 0, 0))
    x3 = send(own, 0, -1, named("pqb", 0, 0))
    (four,) = pack([(two, 0, 2), (pair_swap(two, 4), 0, 2)])
    (cross,) = cut(named("b", 0, 1))
    x2 = send(cross, 0, 1, named("b", 0, 1))

    pair_orbitals, virtual_pairs = after(pair_orbitals, z1), after(virtual_pairs, z1)
    occupied = table_lookup(occupied_energy, pair_orbitals.reshape(-1)).reshape(2, -1)
    virtual = table_lookup(virtual_energy, virtual_pairs.reshape(-1)).reshape(2, -1)
    pair_energy = (occupied[0] + occupied[1])[:, None]
    virtual_sum = (virtual[0] + virtual[1])[None, :]
    near = named("pq", 1, 0) + named("pq", 3, 0)
    up_keys, down_keys = [(1, 0, "p"), (0, 0, "b")], [(3, 0, "q"), (0, 0, "b")]
    up, down, sides = cut(up_keys, down_keys, near)
    up, down, sides, four = barrier(up, down, sides, four, z1, z3, x1, x3, x2)[:4]
    far_four = opposite_y(four)
    z1 = send(up, 1, 0, up_keys)
    z3 = send(down, -1, 0, down_keys)
    x1 = send(sides, 0, 1, near)
    x3 = send(sides, 0, -1, near)
    crossing = named("b", 0, 1) + named("b", 0, 3) + named("b", 0, 2)
    (crossing_rows,) = cut(crossing)
    right_keys = named("pq", 2, 0) + named("pq", 1, 1)
    left_keys = named("pq", 2, 0) + named("pq", 3, 3)
    right, left = cut(right_keys, left_keys)
    crossing_rows, right, left, far_four, pair_energy, virtual_sum = barrier(
        crossing_rows, right, left, far_four, pair_energy, virtual_sum, z1, z3, x1, x3
    )[:6]
    far_other = pair_swap(far_four, 1)
    z1 = send(crossing_rows, 1, 0, crossing)
    z3 = send(crossing_rows, -1, 0, crossing)
    x1 = send(right, 0, 1, right_keys)
    x3 = send(left, 0, -1, left_keys)

    def planned(*segments):
        plan, pieces = [], []
        for segment, slot, names in segments:
            parts = []
            for name in names:
                array, at = have[name + (segment,)]
                known = [i for i, piece in enumerate(pieces) if piece is array]
                if not known:
                    pieces.append(array)
                parts.append((known[0] if known else len(pieces) - 1, at))
            start = {"p": 0, "q": part, "b": whole}[segment]
            plan.append((start, size[segment], slot, tuple(parts)))
        return tuple(plan), pieces

    up_keys, down_keys = [(1, 0, "b"), (1, 1, "b")], [(3, 3, "b"), (3, 2, "b")]
    right_keys, left_keys = [(2, 1, "p"), (0, 1, "p")], [(2, 3, "q"), (0, 3, "q")]
    up, down, right, left = cut(up_keys, down_keys, right_keys, left_keys)
    up, down, right, left, four, far_other = barrier(
        up, down, right, left, four, far_other, z1, z3, x1, x3
    )[:6]
    other_four = pair_swap(four, 1)
    send(up, 1, 0, up_keys)
    send(down, -1, 0, down_keys)
    send(right, 0, 1, right_keys)
    send(left, 0, -1, left_keys)

    total, tail = early_matmul(
        where,
        integral_cols,
        live_slots,
        [four, other_four, far_four, far_other],
        *planned(("p", 0, ORDER[:14]), ("q", 0, ORDER[:14]), ("b", 3, ORDER[3:15])),
    )
    last = [(2, 2), (0, 2)]
    return late_matmul(
        tail,
        total,
        (virtual_sum, pair_energy),
        *planned(("p", 3, last), ("q", 3, last), ("b", 0, [(2, 0), (2, 1), (2, 3), (2, 2)])),
    )


def solution(mesh):
    placed = (
        P("pair", "virt"),
        P("pair", "virt"),
        P("virt", "pair", None, None),
        P("virt", None),
        P("virt"),
        P(None, "pair"),
        P(None, "virt"),
        P(),
        P(),
    )
    return jax.shard_map(
        per_device, mesh=mesh, in_specs=placed, out_specs=P("pair", "virt"), check_vma=False
    )
```

```python
import functools

import jax
import jax.numpy as jnp
import numpy as np
from jax import lax
from jax.experimental import pallas as pl
from jax.experimental.pallas import tpu as pltpu
from jax.sharding import PartitionSpec as P

ANY = pl.BlockSpec(memory_space=pl.ANY)
SMEM = pl.BlockSpec(memory_space=pltpu.SMEM)
VMEM = pl.BlockSpec(memory_space=pltpu.VMEM)
EARLY_VMEM = 30 * 1024 * 1024
LATE_VMEM = 16 * 1024 * 1024
RING = 4
CROSS_ROWS = 320
GROUP = 5
ORDER = (
    [(2, 0), (2, 1), (2, 3)]
    + [(0, 0), (0, 1), (0, 3), (1, 0), (3, 0), (1, 1), (1, 3), (3, 1), (3, 3), (1, 2), (3, 2)]
    + [(0, 2), (2, 2)]
)
TAIL_SLOTS = (0, 1, 2, 15, 14)


def slot_table():
    table = np.zeros((16, 16), np.int32)
    for pair in range(16):
        y, zlo, core = pair // 4, pair // 2 % 2, pair % 2
        for local in range(16):
            far, swapped, near = local // 8, local // 4 % 2, local // 2 % 2
            other_y = (y + 2 * far) % 4 ^ near
            table[pair, local] = other_y * 4 + (zlo ^ local % 2) * 2 + (core ^ swapped)
    return table


def order_table():
    table = np.zeros((16, 16), np.int32)
    for virt in range(RING * RING):
        for place, (dz, dx) in enumerate(ORDER):
            table[virt, (virt // RING - dz) % RING * RING + (virt % RING - dx) % RING] = place
    return table


def barrier(*arrays):
    return lax.optimization_barrier(arrays)


def after(array, *first):
    return lax.optimization_barrier((array,) + first)[0]


def virt_shift(array, dz, dx):
    pairs = [
        (z * RING + x, (z + dz) % RING * RING + (x + dx) % RING)
        for z in range(RING)
        for x in range(RING)
    ]
    return lax.ppermute(array, "virt", pairs)


def pair_swap(array, bit):
    return lax.ppermute(array, "pair", [(i, i ^ bit) for i in range(16)])


def opposite_y(array):
    return lax.ppermute(array, "pair", [(i, (i + 8) % 16) for i in range(16)])


def table_lookup(table, index):
    rows = -(-table.shape[0] // 128)
    padded = jnp.zeros((rows * 128,), jnp.float32).at[: table.shape[0]].set(table).reshape(rows, 128)
    chosen = (index[:, None] // 128 == jnp.arange(rows, dtype=jnp.int32)[None, :]).astype(jnp.float32)
    lines = jnp.dot(chosen, padded, precision=lax.Precision.HIGHEST)
    lane = index[:, None] % 128 == jnp.arange(128, dtype=jnp.int32)[None, :]
    return jnp.sum(jnp.where(lane, lines, 0.0), axis=1)


def mask_kernel(whole, amp_map, amplitudes, masked, front):
    for tile in range(amp_map.shape[1]):
        for column in range(amp_map.shape[0]):
            keep = amp_map[column, tile].astype(jnp.float32).astype(jnp.bfloat16)
            block = (slice(tile * 128, tile * 128 + 128), slice(column * 128, column * 128 + 128))
            masked[block] = amplitudes[block] * keep
    front[...] = masked[:whole]


def mask(amplitudes, amp_map, whole):
    rows, columns = amplitudes.shape
    return pl.pallas_call(
        functools.partial(mask_kernel, whole),
        in_specs=[SMEM, VMEM],
        out_specs=[VMEM] * 2,
        out_shape=[jax.ShapeDtypeStruct((n, columns), jnp.bfloat16) for n in (rows, whole)],
    )(amp_map.T, amplitudes)


def pack_kernel(plan, count, *refs):
    sem = refs[-1]
    copies = []
    for target, parts in zip(refs[count:-1], plan):
        at = 0
        for source, first, size in parts:
            copies.append(
                pltpu.make_async_copy(
                    refs[source].at[pl.ds(first, size)], target.at[pl.ds(at, size)], sem.at[len(copies)]
                )
            )
            at += size
    for copy in copies:
        copy.start()
    for copy in copies:
        copy.wait()


def pack(*lists):
    arrays, plan, shapes = [], [], []
    for parts in lists:
        made = []
        for array, first, size in parts:
            known = [i for i, other in enumerate(arrays) if other is array]
            if not known:
                arrays.append(array)
            made.append((known[0] if known else len(arrays) - 1, first, size))
        plan.append(made)
        shapes.append((sum(size for _, _, size in parts),) + parts[0][0].shape[1:])
    return pl.pallas_call(
        functools.partial(pack_kernel, plan, len(arrays)),
        in_specs=[ANY] * len(arrays),
        out_specs=[VMEM] * len(shapes),
        out_shape=[jax.ShapeDtypeStruct(shape, jnp.bfloat16) for shape in shapes],
        scratch_shapes=[pltpu.SemaphoreType.DMA((sum(len(parts) for parts in plan),))],
        cost_estimate=pl.CostEstimate(
            flops=0, bytes_accessed=sum(2 * int(np.prod(shape)) for shape in shapes), transcendentals=0
        ),
    )(*arrays)


def segment_dot(held, arrived, weights, first_slot, count, target):
    for group in range(0, count, GROUP):
        last = min(group + GROUP, count)
        for j in range(group, last):
            arrived(j)
        part = jnp.dot(
            held[:, group * 256 : last * 256],
            weights[(first_slot + group) * 256 : (first_slot + last) * 256, :],
            preferred_element_type=jnp.float32,
        )
        target[...] = part if group == 0 else target[...] + part


def start_blocks(plan, pieces, held, held_sem):
    for s, (_, _, _, parts) in enumerate(plan):
        for j, copies in enumerate(parts):
            for piece, first, start, count in copies:
                pltpu.make_async_copy(
                    pieces[piece].at[pl.ds(first, count)],
                    held[s].at[pl.ds(start, count), pl.ds(j * 256, 256)],
                    held_sem[s].at[j],
                ).start()


def block_waiter(held, sem):
    def wait(j):
        slot = held.at[:, pl.ds(j * 256, 256)]
        pltpu.make_async_copy(slot, slot, sem.at[j]).wait()

    return wait


def early_kernel(plan, tile_count, piece_count, where, cols, live, *refs):
    sources, refs = refs[:tile_count], refs[tile_count:]
    pieces = refs[:piece_count]
    total, tail, weights, tiles, tile_sem = refs[piece_count : piece_count + 5]
    rest = refs[piece_count + 5 :]
    held, held_sem = rest[: len(plan)], rest[len(plan) :]
    slots = tiles.shape[0]
    each = slots // tile_count
    loads = [
        pltpu.make_async_copy(source, tiles.at[pl.ds(i * each, each)], tile_sem.at[i])
        for i, source in enumerate(sources)
    ]
    for load in loads:
        load.start()
    start_blocks(plan, pieces, held, held_sem)
    weights[...] = jnp.zeros_like(weights)
    for load in loads:
        load.wait()
    for k in range(cols.shape[0]):

        def place(local, carry, k=k):
            slot = where[local]

            @pl.when(slot < live[k])
            def _():
                column = cols[k, slot]
                row = where[slots + column // 2] * 256 + column % 2 * 128
                weights[pl.ds(pl.multiple_of(row, 128), 128), k * 128 : k * 128 + 128] = tiles[local, k]

            return carry

        lax.fori_loop(0, slots, place, 0)
    for i, slot in enumerate(TAIL_SLOTS):
        tail[i * 256 : i * 256 + 256, :] = weights[slot * 256 : slot * 256 + 256, :]
    for s, (first_row, rows, first_slot, parts) in enumerate(plan):
        target = total.at[pl.ds(first_row, rows)]
        segment_dot(
            held[s], block_waiter(held[s], held_sem[s]), weights, first_slot, len(parts), target
        )


def late_kernel(plan, piece_count, weights, total, virtual_sum, pair_energy, *refs):
    pieces = refs[:piece_count]
    out, staged, out_sem = refs[piece_count : piece_count + 3]
    rest = refs[piece_count + 3 :]
    held, held_sem = rest[: len(plan)], rest[len(plan) :]
    start_blocks(plan, pieces, held, held_sem)
    stores = []
    for s, (first_row, rows, first_slot, parts) in enumerate(plan):
        span = slice(first_row, first_row + rows)
        count = len(parts)
        for j in range(count):
            block_waiter(held[s], held_sem[s])(j)
        product = total[span, :] + jnp.dot(
            held[s][...],
            weights[first_slot * 256 : (first_slot + count) * 256, :],
            preferred_element_type=jnp.float32,
        )
        staged[span, :] = (product / (virtual_sum[...] - pair_energy[span, :])).astype(jnp.bfloat16)
        store = pltpu.make_async_copy(
            staged.at[pl.ds(first_row, rows)], out.at[pl.ds(first_row, rows)], out_sem.at[s]
        )
        store.start()
        stores.append(store)
    for store in stores:
        store.wait()


def block_scratch(plan):
    held = [pltpu.VMEM((rows, len(parts) * 256), jnp.bfloat16) for _, rows, _, parts in plan]
    return held + [pltpu.SemaphoreType.DMA((len(parts),)) for _, _, _, parts in plan]


def cost(plan, columns, extra):
    work = sum(rows * len(parts) for _, rows, _, parts in plan)
    return pl.CostEstimate(flops=2 * work * 256 * columns, bytes_accessed=work * 512 + extra, transcendentals=0)


def early_matmul(where, cols, live, tiles, plan, pieces):
    columns = cols.shape[0] * 128
    all_rows = sum(rows for _, rows, _, _ in plan)
    return pl.pallas_call(
        functools.partial(early_kernel, plan, len(tiles), len(pieces)),
        in_specs=[SMEM] * 3 + [ANY] * (len(tiles) + len(pieces)),
        out_specs=[VMEM, VMEM],
        out_shape=[
            jax.ShapeDtypeStruct((all_rows, columns), jnp.float32),
            jax.ShapeDtypeStruct((len(TAIL_SLOTS) * 256, columns), jnp.bfloat16),
        ],
        scratch_shapes=[
            pltpu.VMEM((16 * 256, columns), jnp.bfloat16),
            pltpu.VMEM((16,) + tiles[0].shape[1:], jnp.bfloat16),
            pltpu.SemaphoreType.DMA((len(tiles),)),
        ]
        + block_scratch(plan),
        cost_estimate=cost(plan, columns, 16 * 2**20),
        compiler_params=pltpu.CompilerParams(vmem_limit_bytes=EARLY_VMEM),
    )(where, cols, live, *tiles, *pieces)


def late_matmul(weights, total, energies, plan, pieces):
    rows, columns = total.shape
    return pl.pallas_call(
        functools.partial(late_kernel, plan, len(pieces)),
        in_specs=[VMEM] * 4 + [ANY] * len(pieces),
        out_specs=ANY,
        out_shape=jax.ShapeDtypeStruct((rows, columns), jnp.bfloat16),
        scratch_shapes=[
            pltpu.VMEM((rows, columns), jnp.bfloat16),
            pltpu.SemaphoreType.DMA((len(plan),)),
        ]
        + block_scratch(plan),
        cost_estimate=cost(plan, columns, 12 * 2**20),
        compiler_params=pltpu.CompilerParams(vmem_limit_bytes=LATE_VMEM),
    )(weights, total, *energies, *pieces)


def per_device(
    amplitudes,
    amp_map,
    integral_tiles,
    integral_cols,
    live_slots,
    pair_orbitals,
    virtual_pairs,
    occupied_energy,
    virtual_energy,
):
    row_count = amplitudes.shape[0]
    cross = CROSS_ROWS
    part = (row_count - cross) // 2
    whole = row_count - cross
    own, front = mask(amplitudes, amp_map, whole)
    pair = lax.axis_index("pair")
    virt = lax.axis_index("virt")

    spots = np.concatenate(
        [np.repeat(slot_table(), RING * RING, axis=0), np.tile(order_table(), (16, 1))], axis=1
    )
    where = jnp.asarray(spots)[pair * (RING * RING) + virt]

    have = {(0, 0, "p"): (own, 0), (0, 0, "q"): (own, part), (0, 0, "b"): (own, whole)}
    size = {"p": part, "q": part, "b": cross}

    def cut(*lists):
        return pack(*[[have[key] + (size[key[2]],) for key in keys] for keys in lists])

    def arrive(array, keys, dz, dx):
        at = 0
        for z, x, s in keys:
            have[(z + dz) % RING, (x + dx) % RING, s] = (array, at)
            at += size[s]

    def send(array, dz, dx, keys):
        array = virt_shift(array, dz, dx)
        arrive(array, keys, dz, dx)
        return array

    def named(names, z, x):
        return [(z, x, s) for s in names]

    tiles = integral_tiles.reshape((1, integral_tiles.shape[0]) + integral_tiles.shape[2:])
    partner = pair_swap(tiles, 2)
    own, front, partner = barrier(own, front, partner)
    have.update({(0, 0, "p"): (own, 0), (0, 0, "q"): (own, part), (0, 0, "b"): (own, whole)})
    (two,) = pack([(tiles, 0, 1), (partner, 0, 1)])

    z1 = send(front, 1, 0, named("pq", 0, 0))
    z3 = send(front, -1, 0, named("pq", 0, 0))
    x1 = send(own, 0, 1, named("pqb", 0, 0))
    x3 = send(own, 0, -1, named("pqb", 0, 0))
    (four,) = pack([(two, 0, 2), (pair_swap(two, 4), 0, 2)])
    (cross,) = cut(named("b", 0, 1))
    x2 = send(cross, 0, 1, named("b", 0, 1))

    pair_orbitals, virtual_pairs = after(pair_orbitals, z1), after(virtual_pairs, z1)
    occupied = table_lookup(occupied_energy, pair_orbitals.reshape(-1)).reshape(2, -1)
    virtual = table_lookup(virtual_energy, virtual_pairs.reshape(-1)).reshape(2, -1)
    pair_energy = (occupied[0] + occupied[1])[:, None]
    virtual_sum = (virtual[0] + virtual[1])[None, :]
    near = named("pq", 1, 0) + named("pq", 3, 0)
    up_keys, down_keys = [(1, 0, "p"), (0, 0, "b")], [(3, 0, "q"), (0, 0, "b")]
    up, down, sides = cut(up_keys, down_keys, near)
    up, down, sides, four = barrier(up, down, sides, four, z1, z3, x1, x3, x2)[:4]
    far_four = opposite_y(four)
    z1 = send(up, 1, 0, up_keys)
    z3 = send(down, -1, 0, down_keys)
    x1 = send(sides, 0, 1, near)
    x3 = send(sides, 0, -1, near)
    crossing = named("b", 0, 1) + named("b", 0, 3) + named("b", 0, 2)
    (crossing_rows,) = cut(crossing)
    right_keys = named("pq", 2, 0) + named("pq", 1, 1)
    left_keys = named("pq", 2, 0) + named("pq", 3, 3)
    right, left = cut(right_keys, left_keys)
    crossing_rows, right, left, far_four, pair_energy, virtual_sum = barrier(
        crossing_rows, right, left, far_four, pair_energy, virtual_sum, z1, z3, x1, x3
    )[:6]
    far_other = pair_swap(far_four, 1)
    z1 = send(crossing_rows, 1, 0, crossing)
    z3 = send(crossing_rows, -1, 0, crossing)
    x1 = send(right, 0, 1, right_keys)
    x3 = send(left, 0, -1, left_keys)

    def planned(*segments):
        plan, pieces = [], []
        begin = {"p": 0, "q": part, "b": whole}
        for letters, slot, names in segments:
            parts = []
            for name in names:
                copies = []
                for letter in letters:
                    array, at = have[name + (letter,)]
                    known = [i for i, piece in enumerate(pieces) if piece is array]
                    if not known:
                        pieces.append(array)
                    piece = known[0] if known else len(pieces) - 1
                    start = begin[letter] - begin[letters[0]]
                    if copies and copies[-1][0] == piece and copies[-1][1] + copies[-1][3] == at:
                        copies[-1] = copies[-1][:3] + (copies[-1][3] + size[letter],)
                    else:
                        copies.append((piece, at, start, size[letter]))
                parts.append(tuple(copies))
            rows = sum(size[letter] for letter in letters)
            plan.append((begin[letters[0]], rows, slot, tuple(parts)))
        return tuple(plan), pieces

    up_keys, down_keys = [(1, 0, "b"), (1, 1, "b")], [(3, 3, "b"), (3, 2, "b")]
    right_keys, left_keys = [(2, 1, "p"), (0, 1, "p")], [(2, 3, "q"), (0, 3, "q")]
    up, down, right, left = cut(up_keys, down_keys, right_keys, left_keys)
    up, down, right, left, four, far_other = barrier(
        up, down, right, left, four, far_other, z1, z3, x1, x3
    )[:6]
    other_four = pair_swap(four, 1)
    send(up, 1, 0, up_keys)
    send(down, -1, 0, down_keys)
    send(right, 0, 1, right_keys)
    send(left, 0, -1, left_keys)

    total, tail = early_matmul(
        where,
        integral_cols,
        live_slots,
        [four, other_four, far_four, far_other],
        *planned(("pq", 0, ORDER[:14]), ("b", 3, ORDER[3:15])),
    )
    last = [(2, 2), (0, 2)]
    return late_matmul(
        tail,
        total,
        (virtual_sum, pair_energy),
        *planned(("pq", 3, last), ("b", 0, [(2, 0), (2, 1), (2, 3), (2, 2)])),
    )


def solution(mesh):
    placed = (
        P("pair", "virt"),
        P("pair", "virt"),
        P("virt", "pair", None, None),
        P("virt", None),
        P("virt"),
        P(None, "pair"),
        P(None, "virt"),
        P(),
        P(),
    )
    return jax.shard_map(
        per_device, mesh=mesh, in_specs=placed, out_specs=P("pair", "virt"), check_vma=False
    )
```

```python
import functools

import jax
import jax.numpy as jnp
import numpy as np
from jax import lax
from jax.experimental import pallas as pl
from jax.experimental.pallas import tpu as pltpu
from jax.sharding import PartitionSpec as P

ANY = pl.BlockSpec(memory_space=pl.ANY)
SMEM = pl.BlockSpec(memory_space=pltpu.SMEM)
VMEM = pl.BlockSpec(memory_space=pltpu.VMEM)
EARLY_VMEM = 30 * 1024 * 1024
LATE_VMEM = 16 * 1024 * 1024
RING = 4
CROSS_ROWS = 320
GROUP = 7
ORDER = (
    [(2, 0), (2, 1), (2, 3)]
    + [(0, 0), (0, 1), (0, 3), (1, 0), (3, 0), (1, 1), (1, 3), (3, 1), (3, 3), (1, 2), (3, 2)]
    + [(0, 2), (2, 2)]
)
TAIL_SLOTS = (0, 1, 2, 15, 14)


def slot_table():
    table = np.zeros((16, 16), np.int32)
    for pair in range(16):
        y, zlo, core = pair // 4, pair // 2 % 2, pair % 2
        for local in range(16):
            far, swapped, near = local // 8, local // 4 % 2, local // 2 % 2
            other_y = (y + 2 * far) % 4 ^ near
            table[pair, local] = other_y * 4 + (zlo ^ local % 2) * 2 + (core ^ swapped)
    return table


def order_table():
    table = np.zeros((16, 16), np.int32)
    for virt in range(RING * RING):
        for place, (dz, dx) in enumerate(ORDER):
            table[virt, (virt // RING - dz) % RING * RING + (virt % RING - dx) % RING] = place
    return table


def barrier(*arrays):
    return lax.optimization_barrier(arrays)


def after(array, *first):
    return lax.optimization_barrier((array,) + first)[0]


def virt_shift(array, dz, dx):
    pairs = [
        (z * RING + x, (z + dz) % RING * RING + (x + dx) % RING)
        for z in range(RING)
        for x in range(RING)
    ]
    return lax.ppermute(array, "virt", pairs)


def pair_swap(array, bit):
    return lax.ppermute(array, "pair", [(i, i ^ bit) for i in range(16)])


def opposite_y(array):
    return lax.ppermute(array, "pair", [(i, (i + 8) % 16) for i in range(16)])


def table_lookup(table, index):
    rows = -(-table.shape[0] // 128)
    padded = jnp.zeros((rows * 128,), jnp.float32).at[: table.shape[0]].set(table).reshape(rows, 128)
    chosen = (index[:, None] // 128 == jnp.arange(rows, dtype=jnp.int32)[None, :]).astype(jnp.float32)
    lines = jnp.dot(chosen, padded, precision=lax.Precision.HIGHEST)
    lane = index[:, None] % 128 == jnp.arange(128, dtype=jnp.int32)[None, :]
    return jnp.sum(jnp.where(lane, lines, 0.0), axis=1)


def mask_kernel(whole, amp_map, amplitudes, masked, front):
    for tile in range(amp_map.shape[1]):
        for column in range(amp_map.shape[0]):
            keep = amp_map[column, tile].astype(jnp.float32).astype(jnp.bfloat16)
            block = (slice(tile * 128, tile * 128 + 128), slice(column * 128, column * 128 + 128))
            masked[block] = amplitudes[block] * keep
    front[...] = masked[:whole]


def mask(amplitudes, amp_map, whole):
    rows, columns = amplitudes.shape
    return pl.pallas_call(
        functools.partial(mask_kernel, whole),
        in_specs=[SMEM, VMEM],
        out_specs=[VMEM] * 2,
        out_shape=[jax.ShapeDtypeStruct((n, columns), jnp.bfloat16) for n in (rows, whole)],
    )(amp_map.T, amplitudes)


def pack_kernel(plan, count, *refs):
    sem = refs[-1]
    copies = []
    for target, parts in zip(refs[count:-1], plan):
        at = 0
        for source, first, size in parts:
            copies.append(
                pltpu.make_async_copy(
                    refs[source].at[pl.ds(first, size)], target.at[pl.ds(at, size)], sem.at[len(copies)]
                )
            )
            at += size
    for copy in copies:
        copy.start()
    for copy in copies:
        copy.wait()


def pack(*lists):
    arrays, plan, shapes = [], [], []
    for parts in lists:
        made = []
        for array, first, size in parts:
            known = [i for i, other in enumerate(arrays) if other is array]
            if not known:
                arrays.append(array)
            made.append((known[0] if known else len(arrays) - 1, first, size))
        plan.append(made)
        shapes.append((sum(size for _, _, size in parts),) + parts[0][0].shape[1:])
    return pl.pallas_call(
        functools.partial(pack_kernel, plan, len(arrays)),
        in_specs=[ANY] * len(arrays),
        out_specs=[VMEM] * len(shapes),
        out_shape=[jax.ShapeDtypeStruct(shape, jnp.bfloat16) for shape in shapes],
        scratch_shapes=[pltpu.SemaphoreType.DMA((sum(len(parts) for parts in plan),))],
        cost_estimate=pl.CostEstimate(
            flops=0, bytes_accessed=sum(2 * int(np.prod(shape)) for shape in shapes), transcendentals=0
        ),
    )(*arrays)


def segment_dot(held, arrived, weights, first_slot, count, target):
    for group in range(0, count, GROUP):
        last = min(group + GROUP, count)
        for j in range(group, last):
            arrived(j)
        part = jnp.dot(
            held[:, group * 256 : last * 256],
            weights[(first_slot + group) * 256 : (first_slot + last) * 256, :],
            preferred_element_type=jnp.float32,
        )
        target[...] = part if group == 0 else target[...] + part


def start_blocks(plan, pieces, held, held_sem):
    for s, (_, _, _, parts) in enumerate(plan):
        for j, copies in enumerate(parts):
            for piece, first, start, count in copies:
                pltpu.make_async_copy(
                    pieces[piece].at[pl.ds(first, count)],
                    held[s].at[pl.ds(start, count), pl.ds(j * 256, 256)],
                    held_sem[s].at[j],
                ).start()


def block_waiter(held, sem):
    def wait(j):
        slot = held.at[:, pl.ds(j * 256, 256)]
        pltpu.make_async_copy(slot, slot, sem.at[j]).wait()

    return wait


def early_kernel(plan, tile_count, piece_count, where, cols, live, *refs):
    sources, refs = refs[:tile_count], refs[tile_count:]
    pieces = refs[:piece_count]
    total, tail, weights, tiles, tile_sem = refs[piece_count : piece_count + 5]
    rest = refs[piece_count + 5 :]
    held, held_sem = rest[: len(plan)], rest[len(plan) :]
    slots = tiles.shape[0]
    each = slots // tile_count
    loads = [
        pltpu.make_async_copy(source, tiles.at[pl.ds(i * each, each)], tile_sem.at[i])
        for i, source in enumerate(sources)
    ]
    for load in loads:
        load.start()
    start_blocks(plan, pieces, held, held_sem)
    weights[...] = jnp.zeros_like(weights)
    for load in loads:
        load.wait()
    for k in range(cols.shape[0]):

        def place(local, carry, k=k):
            slot = where[local]

            @pl.when(slot < live[k])
            def _():
                column = cols[k, slot]
                row = where[slots + column // 2] * 256 + column % 2 * 128
                weights[pl.ds(pl.multiple_of(row, 128), 128), k * 128 : k * 128 + 128] = tiles[local, k]

            return carry

        lax.fori_loop(0, slots, place, 0)
    for i, slot in enumerate(TAIL_SLOTS):
        tail[i * 256 : i * 256 + 256, :] = weights[slot * 256 : slot * 256 + 256, :]
    for s, (first_row, rows, first_slot, parts) in enumerate(plan):
        target = total.at[pl.ds(first_row, rows)]
        segment_dot(
            held[s], block_waiter(held[s], held_sem[s]), weights, first_slot, len(parts), target
        )


def late_kernel(plan, piece_count, weights, total, virtual_sum, pair_energy, *refs):
    pieces = refs[:piece_count]
    out, staged, out_sem = refs[piece_count : piece_count + 3]
    rest = refs[piece_count + 3 :]
    held, held_sem = rest[: len(plan)], rest[len(plan) :]
    start_blocks(plan, pieces, held, held_sem)
    stores = []
    for s, (first_row, rows, first_slot, parts) in enumerate(plan):
        span = slice(first_row, first_row + rows)
        count = len(parts)
        for j in range(count):
            block_waiter(held[s], held_sem[s])(j)
        product = total[span, :] + jnp.dot(
            held[s][...],
            weights[first_slot * 256 : (first_slot + count) * 256, :],
            preferred_element_type=jnp.float32,
        )
        staged[span, :] = (product / (virtual_sum[...] - pair_energy[span, :])).astype(jnp.bfloat16)
        store = pltpu.make_async_copy(
            staged.at[pl.ds(first_row, rows)], out.at[pl.ds(first_row, rows)], out_sem.at[s]
        )
        store.start()
        stores.append(store)
    for store in stores:
        store.wait()


def block_scratch(plan):
    held = [pltpu.VMEM((rows, len(parts) * 256), jnp.bfloat16) for _, rows, _, parts in plan]
    return held + [pltpu.SemaphoreType.DMA((len(parts),)) for _, _, _, parts in plan]


def cost(plan, columns, extra):
    work = sum(rows * len(parts) for _, rows, _, parts in plan)
    return pl.CostEstimate(flops=2 * work * 256 * columns, bytes_accessed=work * 512 + extra, transcendentals=0)


def early_matmul(where, cols, live, tiles, plan, pieces):
    columns = cols.shape[0] * 128
    all_rows = sum(rows for _, rows, _, _ in plan)
    return pl.pallas_call(
        functools.partial(early_kernel, plan, len(tiles), len(pieces)),
        in_specs=[SMEM] * 3 + [ANY] * (len(tiles) + len(pieces)),
        out_specs=[VMEM, VMEM],
        out_shape=[
            jax.ShapeDtypeStruct((all_rows, columns), jnp.float32),
            jax.ShapeDtypeStruct((len(TAIL_SLOTS) * 256, columns), jnp.bfloat16),
        ],
        scratch_shapes=[
            pltpu.VMEM((16 * 256, columns), jnp.bfloat16),
            pltpu.VMEM((16,) + tiles[0].shape[1:], jnp.bfloat16),
            pltpu.SemaphoreType.DMA((len(tiles),)),
        ]
        + block_scratch(plan),
        cost_estimate=cost(plan, columns, 16 * 2**20),
        compiler_params=pltpu.CompilerParams(vmem_limit_bytes=EARLY_VMEM),
    )(where, cols, live, *tiles, *pieces)


def late_matmul(weights, total, energies, plan, pieces):
    rows, columns = total.shape
    return pl.pallas_call(
        functools.partial(late_kernel, plan, len(pieces)),
        in_specs=[VMEM] * 4 + [ANY] * len(pieces),
        out_specs=ANY,
        out_shape=jax.ShapeDtypeStruct((rows, columns), jnp.bfloat16),
        scratch_shapes=[
            pltpu.VMEM((rows, columns), jnp.bfloat16),
            pltpu.SemaphoreType.DMA((len(plan),)),
        ]
        + block_scratch(plan),
        cost_estimate=cost(plan, columns, 12 * 2**20),
        compiler_params=pltpu.CompilerParams(vmem_limit_bytes=LATE_VMEM),
    )(weights, total, *energies, *pieces)


def per_device(
    amplitudes,
    amp_map,
    integral_tiles,
    integral_cols,
    live_slots,
    pair_orbitals,
    virtual_pairs,
    occupied_energy,
    virtual_energy,
):
    row_count = amplitudes.shape[0]
    cross = CROSS_ROWS
    part = (row_count - cross) // 2
    whole = row_count - cross
    own, front = mask(amplitudes, amp_map, whole)
    pair = lax.axis_index("pair")
    virt = lax.axis_index("virt")

    spots = np.concatenate(
        [np.repeat(slot_table(), RING * RING, axis=0), np.tile(order_table(), (16, 1))], axis=1
    )
    where = jnp.asarray(spots)[pair * (RING * RING) + virt]

    have = {(0, 0, "p"): (own, 0), (0, 0, "q"): (own, part), (0, 0, "b"): (own, whole)}
    size = {"p": part, "q": part, "b": cross}

    def cut(*lists):
        return pack(*[[have[key] + (size[key[2]],) for key in keys] for keys in lists])

    def arrive(array, keys, dz, dx):
        at = 0
        for z, x, s in keys:
            have[(z + dz) % RING, (x + dx) % RING, s] = (array, at)
            at += size[s]

    def send(array, dz, dx, keys):
        array = virt_shift(array, dz, dx)
        arrive(array, keys, dz, dx)
        return array

    def named(names, z, x):
        return [(z, x, s) for s in names]

    tiles = integral_tiles.reshape((1, integral_tiles.shape[0]) + integral_tiles.shape[2:])
    partner = pair_swap(tiles, 2)
    own, front, partner = barrier(own, front, partner)
    have.update({(0, 0, "p"): (own, 0), (0, 0, "q"): (own, part), (0, 0, "b"): (own, whole)})
    (two,) = pack([(tiles, 0, 1), (partner, 0, 1)])

    z1 = send(front, 1, 0, named("pq", 0, 0))
    z3 = send(front, -1, 0, named("pq", 0, 0))
    x1 = send(own, 0, 1, named("pqb", 0, 0))
    x3 = send(own, 0, -1, named("pqb", 0, 0))
    (four,) = pack([(two, 0, 2), (pair_swap(two, 4), 0, 2)])
    (cross,) = cut(named("b", 0, 1))
    x2 = send(cross, 0, 1, named("b", 0, 1))

    pair_orbitals, virtual_pairs = after(pair_orbitals, z1), after(virtual_pairs, z1)
    occupied = table_lookup(occupied_energy, pair_orbitals.reshape(-1)).reshape(2, -1)
    virtual = table_lookup(virtual_energy, virtual_pairs.reshape(-1)).reshape(2, -1)
    pair_energy = (occupied[0] + occupied[1])[:, None]
    virtual_sum = (virtual[0] + virtual[1])[None, :]
    near = named("pq", 1, 0) + named("pq", 3, 0)
    up_keys, down_keys = [(1, 0, "p"), (0, 0, "b")], [(3, 0, "q"), (0, 0, "b")]
    up, down, sides = cut(up_keys, down_keys, near)
    up, down, sides, four = barrier(up, down, sides, four, z1, z3, x1, x3, x2)[:4]
    far_four = opposite_y(four)
    z1 = send(up, 1, 0, up_keys)
    z3 = send(down, -1, 0, down_keys)
    x1 = send(sides, 0, 1, near)
    x3 = send(sides, 0, -1, near)
    crossing = named("b", 0, 1) + named("b", 0, 3) + named("b", 0, 2)
    (crossing_rows,) = cut(crossing)
    right_keys = named("pq", 2, 0) + named("pq", 1, 1)
    left_keys = named("pq", 2, 0) + named("pq", 3, 3)
    right, left = cut(right_keys, left_keys)
    crossing_rows, right, left, far_four, pair_energy, virtual_sum = barrier(
        crossing_rows, right, left, far_four, pair_energy, virtual_sum, z1, z3, x1, x3
    )[:6]
    far_other = pair_swap(far_four, 1)
    z1 = send(crossing_rows, 1, 0, crossing)
    z3 = send(crossing_rows, -1, 0, crossing)
    x1 = send(right, 0, 1, right_keys)
    x3 = send(left, 0, -1, left_keys)

    def planned(*segments):
        plan, pieces = [], []
        begin = {"p": 0, "q": part, "b": whole}
        for letters, slot, names in segments:
            parts = []
            for name in names:
                copies = []
                for letter in letters:
                    array, at = have[name + (letter,)]
                    known = [i for i, piece in enumerate(pieces) if piece is array]
                    if not known:
                        pieces.append(array)
                    piece = known[0] if known else len(pieces) - 1
                    start = begin[letter] - begin[letters[0]]
                    if copies and copies[-1][0] == piece and copies[-1][1] + copies[-1][3] == at:
                        copies[-1] = copies[-1][:3] + (copies[-1][3] + size[letter],)
                    else:
                        copies.append((piece, at, start, size[letter]))
                parts.append(tuple(copies))
            rows = sum(size[letter] for letter in letters)
            plan.append((begin[letters[0]], rows, slot, tuple(parts)))
        return tuple(plan), pieces

    up_keys, down_keys = [(1, 0, "b"), (1, 1, "b")], [(3, 3, "b"), (3, 2, "b")]
    right_keys, left_keys = [(2, 1, "p"), (0, 1, "p")], [(2, 3, "q"), (0, 3, "q")]
    up, down, right, left = cut(up_keys, down_keys, right_keys, left_keys)
    up, down, right, left, four, far_other = barrier(
        up, down, right, left, four, far_other, z1, z3, x1, x3
    )[:6]
    other_four = pair_swap(four, 1)
    send(up, 1, 0, up_keys)
    send(down, -1, 0, down_keys)
    send(right, 0, 1, right_keys)
    send(left, 0, -1, left_keys)

    total, tail = early_matmul(
        where,
        integral_cols,
        live_slots,
        [four, other_four, far_four, far_other],
        *planned(("pq", 0, ORDER[:14]), ("b", 3, ORDER[3:15])),
    )
    last = [(2, 2), (0, 2)]
    return late_matmul(
        tail,
        total,
        (virtual_sum, pair_energy),
        *planned(("pq", 3, last), ("b", 0, [(2, 0), (2, 1), (2, 3), (2, 2)])),
    )


def solution(mesh):
    placed = (
        P("pair", "virt"),
        P("pair", "virt"),
        P("virt", "pair", None, None),
        P("virt", None),
        P("virt"),
        P(None, "pair"),
        P(None, "virt"),
        P(),
        P(),
    )
    return jax.shard_map(
        per_device, mesh=mesh, in_specs=placed, out_specs=P("pair", "virt"), check_vma=False
    )
```
